256 devices in a mesh: ctx: 64 (over y, z, core), head: 4 (over x).
Axes of the slice: x: 4, y: 4, z: 8, core: 2. Of those that a mesh axis runs over, the one named last changes fastest.
Arguments:
- main_queries: bfloat16 [8192, 64, 576], P('ctx', 'head'), may hold values from -3.5 to 3.5
- latents: bfloat16 [8192, 576], P('ctx'), may hold values from -3.5 to 3.5
- main_lse: float32 [8192, 64], P('ctx', 'head'), may hold values from -20 to 40, as said below
- index_queries: bfloat16 [8192, 32, 128], P('ctx', 'head'), may hold values from -2 to 2
- index_keys: bfloat16 [8192, 128], P('ctx'), may hold values from -1.5 to 1.5
- index_weights: float32 [8192, 32], P('ctx', 'head'), may hold values from -3 to 3
Outputs:
- loss: float32 [], replicated
- index_query_grads: float32 [8192, 32, 128], P('ctx', 'head')
- index_weight_grads: float32 [8192, 32], P('ctx', 'head')
- index_key_grads: float32 [8192, 128], P(('ctx', 'head'))
The draws below stay inside these ranges and needn't reach their ends.
Inputs may be any that keep to these rules, and one draw needn't show every extreme that they name: main_lse[t, h] is at least the logarithm of the sum over s <= t of exp(S[t, h, s]), so every term of masses is at most 1.
All inputs are finite; a program needn't handle non-finite values.
Results may differ from the reference program's by a relative error of at most 0.021.
Values may be sent and summed in bfloat16 or wider, within the bound.
No kernel may reach another device: no remote copies, remote signals or barrier semaphores. Data moves between devices by JAX's collectives and lax.ppermute only.
A program may use at most 128 MiB of HBM per device.

```python
import jax
import jax.numpy as jnp
from jax import lax

HEADS = 64
LATENT = 512
ROPE = 64
IHEADS = 32
IDIM = 128
TOK_DEV = 128
TOKENS = 8192
N_CTX = 64


score_scale = 192.0 ** (-0.5)


normal_edge = 3.29


def unit_normal(key, array_shape, blend_share):
    bell_curve = jax.random.truncated_normal(jax.random.fold_in(key, 7), -normal_edge, normal_edge, array_shape, jnp.float32)
    uniform_level = jax.random.uniform(jax.random.fold_in(key, 8), array_shape, jnp.float32, -0.999, 0.999)
    return (1.0 - blend_share) * bell_curve + blend_share * jnp.sqrt(3.0) * uniform_level


def main_base(key, spread, blend_share):
    queries = unit_normal(jax.random.fold_in(key, 101), (TOKENS, HEADS, LATENT + ROPE), blend_share)
    row_scale = jnp.exp(spread * jax.random.uniform(jax.random.fold_in(key, 102), (TOKENS, HEADS, 1), jnp.float32, -1.0, 1.0))
    queries = 0.6 * queries * row_scale
    latents = unit_normal(jax.random.fold_in(key, 103), (TOKENS, LATENT + ROPE), blend_share)
    token_scale = jnp.exp(0.5 * spread * jax.random.uniform(jax.random.fold_in(key, 104), (TOKENS, 1), jnp.float32, -1.0, 1.0))
    latents = latents * token_scale
    return (queries.astype(jnp.bfloat16), latents.astype(jnp.bfloat16))


def index_base(key, spread, blend_share, align_share):
    key_reach = IDIM ** (-0.25)
    queries = unit_normal(jax.random.fold_in(key, 201), (TOKENS, IHEADS, IDIM), blend_share) * key_reach
    queries = queries * jnp.exp(spread * jax.random.uniform(jax.random.fold_in(key, 202), (TOKENS, IHEADS, 1), jnp.float32, -1.0, 1.0))
    key_table = unit_normal(jax.random.fold_in(key, 203), (TOKENS, IDIM), blend_share) * key_reach
    weights = unit_normal(jax.random.fold_in(key, 204), (TOKENS, IHEADS), blend_share) * 0.8
    anchor_signs = 0.25 * jax.random.rademacher(jax.random.fold_in(key, 205), (3, IDIM), jnp.float32)
    top_rows = TOKENS - 1 - jnp.arange(3)
    anchor_rows = (2 * jnp.arange(3) + 1) * (TOKENS // 8)
    levels = IDIM * jnp.array([1.0, 2.0, 4.0], jnp.float32)
    factors = jnp.ones((3, IDIM), jnp.float32).at[0, 0:2].set(0.0).at[1, 0].set(0.0).at[2, 0].set(0.5)
    anchor = (1.0 - align_share) * key_table[anchor_rows] + align_share * anchor_signs
    key_table = key_table.at[anchor_rows].set(anchor)
    neighbour = (1.0 - align_share) * key_table[anchor_rows + 1] + align_share * anchor_signs * factors
    key_table = key_table.at[anchor_rows + 1].set(neighbour)
    picked = (1.0 - align_share) * weights[top_rows] + align_share * (jnp.abs(weights[top_rows]) + 0.5)
    weights = weights.at[top_rows].set(picked)
    row_gain = levels / (jnp.sum(picked, axis=1) * jnp.sum(anchor_signs * anchor_signs, axis=1))
    aligned = jnp.broadcast_to((row_gain[:, None] * anchor_signs)[:, None, :], (3, IHEADS, IDIM))
    queries = queries.at[top_rows].set((1.0 - align_share) * queries[top_rows] + align_share * aligned)
    return (queries, key_table, weights)


def draw_main_queries(key, part):
    spread, blend_share = (0.0, 0.0)
    queries, latents = main_base(key, spread, blend_share)
    return queries


def draw_latents(key, part):
    spread, blend_share = (0.0, 0.0)
    queries, latents = main_base(key, spread, blend_share)
    return latents


def draw_main_lse(key, part):
    spread, blend_share = (0.0, 0.0)
    queries, latents = main_base(key, spread, blend_share)
    key = jax.random.fold_in(key, 3)
    offset = jax.random.uniform(key, (TOKENS, HEADS), jnp.float32, 0.0, 1.5)
    positions = jnp.arange(TOKENS, dtype=jnp.int32)
    visible = positions[None, :] <= positions[:, None]

    def one_head(head_queries):
        scores = jnp.dot(head_queries, latents.T, preferred_element_type=jnp.float32) * score_scale
        return jax.nn.logsumexp(jnp.where(visible, scores, -jnp.inf), axis=1)
    exact_lse = lax.map(one_head, jnp.transpose(queries, (1, 0, 2)))
    return (exact_lse.T + offset).astype(jnp.float32)


def draw_index_queries(key, part):
    spread, blend_share, align_share = (0.0, 0.0, 0.0)
    queries, key_table, weights = index_base(key, spread, blend_share, align_share)
    return queries.astype(jnp.bfloat16)


def draw_index_keys(key, part):
    spread, blend_share, align_share = (0.0, 0.0, 0.0)
    queries, key_table, weights = index_base(key, spread, blend_share, align_share)
    return key_table.astype(jnp.bfloat16)


def draw_index_weights(key, part):
    spread, blend_share, align_share = (0.0, 0.0, 0.0)
    queries, key_table, weights = index_base(key, spread, blend_share, align_share)
    return weights.astype(jnp.float32)


def setup_inputs(seed: int = 0) -> dict:
    streams_of = jax.random.split(jax.random.key(seed), 7)
    return {
        "main_queries": draw_main_queries(jax.random.fold_in(streams_of[6], 71), 0),
        "latents": draw_latents(jax.random.fold_in(streams_of[6], 71), 0),
        "main_lse": draw_main_lse(jax.random.fold_in(streams_of[6], 71), 0),
        "index_queries": draw_index_queries(jax.random.fold_in(streams_of[6], 71), 0),
        "index_keys": draw_index_keys(jax.random.fold_in(streams_of[6], 71), 0),
        "index_weights": draw_index_weights(jax.random.fold_in(streams_of[6], 71), 0),
    }


score_scale = 192.0 ** -0.5


def reference(main_queries, latents, main_lse, index_queries, index_keys, index_weights):
    key_pos = jnp.arange(TOKENS, dtype=jnp.int32)
    key_table = index_keys.astype(jnp.float32)

    def one_block(carried, block_index):
        key_grads, loss_sum = carried
        first_row = (block_index * TOK_DEV).astype(jnp.int32)
        queries = lax.dynamic_slice_in_dim(main_queries, first_row, TOK_DEV, 0)
        log_norms = lax.dynamic_slice_in_dim(main_lse, first_row, TOK_DEV, 0)
        index_rows = lax.dynamic_slice_in_dim(index_queries, first_row, TOK_DEV, 0).astype(jnp.float32)
        weights = lax.dynamic_slice_in_dim(index_weights, first_row, TOK_DEV, 0)
        row_pos = first_row + jnp.arange(TOK_DEV, dtype=jnp.int32)
        visible = key_pos[None, :] <= row_pos[:, None]

        def add_head(head_index, masses):
            scores = jnp.dot(queries[:, head_index, :], latents.T, preferred_element_type=jnp.float32) * score_scale
            shifted = jnp.where(visible, scores - log_norms[:, head_index][:, None], -1.0e30)
            return masses + jnp.exp(shifted)

        masses = lax.fori_loop(0, HEADS, add_head, jnp.zeros((TOK_DEV, TOKENS), jnp.float32))
        target = masses / jnp.sum(masses, axis=1, keepdims=True)
        raw_scores = jnp.einsum("tjd,sd->tjs", index_rows, key_table)
        logits = jnp.sum(weights[:, :, None] * jnp.maximum(raw_scores, 0.0), axis=1)
        masked = jnp.where(visible, logits, -jnp.inf)
        log_total = jax.nn.logsumexp(masked, axis=1)
        predicted = jnp.where(visible, jnp.exp(masked - log_total[:, None]), 0.0)
        row_loss = log_total - jnp.sum(target * logits, axis=1)
        coefficient = lax.optimization_barrier((predicted - target).astype(jnp.bfloat16)).astype(jnp.float32)
        weight_grads = jnp.sum(coefficient[:, None, :] * jnp.maximum(raw_scores, 0.0), axis=2)
        gated = coefficient[:, None, :] * weights[:, :, None] * jnp.where(raw_scores > 0.0, 1.0, 0.0)
        mixed_terms = lax.optimization_barrier(gated.astype(jnp.bfloat16)).astype(jnp.float32)
        query_grads = jnp.einsum("tjs,sd->tjd", mixed_terms, key_table)
        key_grads = key_grads + jnp.einsum("tjs,tjd->sd", mixed_terms, index_rows)
        return (key_grads, loss_sum + jnp.sum(row_loss)), (query_grads, weight_grads)

    initial = (jnp.zeros((TOKENS, IDIM), jnp.float32), jnp.zeros((), jnp.float32))
    (key_grads, loss_sum), (query_grads, weight_grads) = lax.scan(one_block, initial, jnp.arange(N_CTX, dtype=jnp.int32))
    return (loss_sum / TOKENS, query_grads.reshape(TOKENS, IHEADS, IDIM), weight_grads.reshape(TOKENS, IHEADS), key_grads)
```

```python
import functools
import math

import jax
import jax.numpy as jnp
from jax import lax
from jax.experimental import pallas as pl
from jax.experimental.pallas import tpu as pltpu
from jax.sharding import PartitionSpec as P

f32, bf16 = jnp.float32, jnp.bfloat16
log2e = math.log2(math.e)
scale2 = 192.0 ** (-0.5) * log2e
far_below = -1e30

Y, Z, C, X = 4, 8, 2, 4
KB = 512
BLOCK = 128
PER = KB // BLOCK
LOSS_ROWS = 16


def ctx_groups(kind):
    place = lambda y, z, c: (y * Z + z) * C + c
    if kind == "y":
        return [[place(y, z, c) for y in range(Y)] for z in range(Z) for c in range(C)]
    return [[place(y, z, c) for z in range(Z)] for y in range(Y) for c in range(C)]


def wide(column, times):
    return jnp.concatenate([column] * times, axis=1)


def kernel(
    heads, iheads, starts, q_ref, lse_ref, iq_ref, iqt_ref, w_ref, keys_ref,
    qg_ref, wg_ref, kg_ref, masses, logits, coeffs,
):
    rows = masses.shape[1]
    latent = q_ref.shape[1]
    blocks = masses.shape[0]
    start = starts[0]
    slot = starts[1]
    count = (start + rows - 1) // KB + 1
    head_chunk = 16
    ihead_chunk = 16

    def key_block(kb, first, last):
        return jnp.concatenate([keys_ref[kb * PER + i, first:last, :] for i in range(PER)], axis=1)

    def first_step(kb, carried):
        lat = key_block(kb, 0, latent)
        total = jnp.zeros((rows, KB), f32)
        for part in range(heads // head_chunk):
            at = pl.ds(part * head_chunk * rows, head_chunk * rows)
            scores = jnp.dot(q_ref[at, :], lat, preferred_element_type=f32)
            mass = jnp.exp2(scores * scale2 - wide(lse_ref[at, :], PER))
            total = total + jnp.sum(mass.reshape(head_chunk, rows, KB), axis=0)
        key_pos = kb * KB + lax.broadcasted_iota(jnp.int32, (rows, KB), 1)
        row_pos = start + lax.broadcasted_iota(jnp.int32, (rows, KB), 0)
        visible = key_pos <= row_pos
        masses[kb] = jnp.where(visible, total, 0.0)
        keys = key_block(kb, latent, latent + BLOCK)
        logit = jnp.zeros((rows, KB), f32)
        for part in range(iheads // ihead_chunk):
            at = pl.ds(part * ihead_chunk * rows, ihead_chunk * rows)
            raw = jnp.dot(iq_ref[at, :], keys, preferred_element_type=f32)
            term = wide(w_ref[at, :], PER) * jnp.maximum(raw, 0.0)
            logit = logit + jnp.sum(term.reshape(ihead_chunk, rows, KB), axis=0)
        logits[kb] = jnp.where(visible, logit, far_below)
        return carried

    lax.fori_loop(0, count, first_step, 0)

    def sum_step(kb, carried):
        mass, top = carried
        return (mass + masses[kb], jnp.maximum(top, logits[kb]))

    mass, top = lax.fori_loop(
        0, count, sum_step, (jnp.zeros((rows, KB), f32), jnp.full((rows, KB), far_below, f32))
    )
    inverse = 1.0 / jnp.sum(mass, axis=1, keepdims=True)
    top = jnp.max(top, axis=1, keepdims=True)

    def exp_step(kb, carried):
        return carried + jnp.exp(logits[kb] - top)

    total = lax.fori_loop(0, count, exp_step, jnp.zeros((rows, KB), f32))
    log_total = top + jnp.log(jnp.sum(total, axis=1, keepdims=True))

    def coefficient_step(kb, carried):
        target = masses[kb] * inverse
        logit = logits[kb]
        coeffs[kb] = (jnp.exp(logit - log_total) - target).astype(bf16).astype(f32)
        return carried + target * logit

    cross = lax.fori_loop(0, count, coefficient_step, jnp.zeros((rows, KB), f32))
    loss = jnp.sum(log_total) - jnp.sum(cross)

    qg_ref[...] = jnp.zeros(qg_ref.shape, f32)
    wg_ref[...] = jnp.zeros(wg_ref.shape, f32)
    per_y = blocks * PER // (Y * C)

    def store_key_grads(kb, grads):
        for i in range(PER):
            pair = kb * (PER // 2) + i // 2
            at = pl.ds(pl.multiple_of((pair % per_y) * BLOCK, BLOCK), BLOCK)
            kg_ref[i % 2, pair // per_y, at, :] = grads[:, i * BLOCK : (i + 1) * BLOCK]

    def second_step(kb, carried):
        keys = key_block(kb, latent, latent + BLOCK)
        coefficient = coeffs[kb]
        key_grads = jnp.zeros((BLOCK, KB), f32)
        for part in range(iheads // ihead_chunk):
            at = pl.ds(part * ihead_chunk * rows, ihead_chunk * rows)
            raw = jnp.dot(iq_ref[at, :], keys, preferred_element_type=f32)
            raw = raw.reshape(ihead_chunk, rows, KB)
            weight = wide(w_ref[at, :], PER).reshape(ihead_chunk, rows, KB)
            add = (coefficient[None] * jnp.maximum(raw, 0.0)).reshape(ihead_chunk * rows, KB)
            add = sum(add[:, i * BLOCK : (i + 1) * BLOCK] for i in range(PER))
            wg_ref[at, :] += add
            mixed = jnp.where(raw > 0.0, coefficient[None] * weight, 0.0).astype(bf16)
            mixed = mixed.reshape(ihead_chunk * rows, KB)
            qg_ref[at, :] += lax.dot_general(
                mixed, keys, (((1,), (1,)), ((), ())), preferred_element_type=f32
            )
            key_grads = key_grads + jnp.dot(iqt_ref[:, at], mixed, preferred_element_type=f32)
        store_key_grads(kb, key_grads.astype(bf16))
        return carried

    lax.fori_loop(0, count, second_step, 0)

    def clear_step(kb, carried):
        store_key_grads(kb, jnp.zeros((BLOCK, KB), bf16))
        return carried

    lax.fori_loop(count, blocks, clear_step, 0)

    lane = lax.broadcasted_iota(jnp.int32, (LOSS_ROWS, BLOCK), 1)
    high = loss.astype(bf16).astype(f32)
    middle = (loss - high).astype(bf16).astype(f32)
    low = loss - high - middle
    piece = jnp.where(lane == slot * 3, high, 0.0)
    piece = piece + jnp.where(lane == slot * 3 + 1, middle, 0.0)
    piece = piece + jnp.where(lane == slot * 3 + 2, low, 0.0)
    for c in range(C):
        for y in range(Y):
            kg_ref[c, y, per_y * BLOCK :, :] = piece.astype(bf16)


def fused(start, slot, q, lse, iq, iqt, w, keys, rows, vmem=60 * 2**20):
    heads, iheads = q.shape[0] // rows, iq.shape[0] // rows
    tokens = keys.shape[0] * BLOCK
    blocks = tokens // KB
    per_y = tokens // BLOCK // (Y * C)
    vm = pl.BlockSpec(memory_space=pltpu.VMEM)
    return pl.pallas_call(
        functools.partial(kernel, heads, iheads),
        out_shape=(
            jax.ShapeDtypeStruct((iheads * rows, BLOCK), f32),
            jax.ShapeDtypeStruct((iheads * rows, BLOCK), f32),
            jax.ShapeDtypeStruct((C, Y, per_y * BLOCK + LOSS_ROWS, BLOCK), bf16),
        ),
        in_specs=[pl.BlockSpec(memory_space=pltpu.SMEM)] + [vm] * 6,
        out_specs=(vm, vm, vm),
        scratch_shapes=[pltpu.VMEM((blocks, rows, KB), f32)] * 3,
        compiler_params=pltpu.CompilerParams(vmem_limit_bytes=vmem),
        name="fused",
    )(jnp.stack([start, slot]).astype(jnp.int32), q, lse, iq, iqt, w, keys)


def head_exchange(array):
    return lax.all_to_all(array, "head", 0, 0, tiled=True)


def per_device(main_queries, latents, main_lse, index_queries, index_keys, index_weights):
    shard = latents.shape[0]
    ctx_count = lax.axis_size("ctx")
    all_tokens = shard * ctx_count
    ctx_place, head_place = lax.axis_index("ctx"), lax.axis_index("head")
    core = ctx_place % C
    y_place = ctx_place // (Z * C)
    rows = shard // X

    own = jnp.concatenate([latents, index_keys], axis=1).T
    keys = lax.all_gather(own[None], "ctx", axis=0, tiled=True)

    def by_rows(array):
        heads = array.shape[1]
        blocks = array.reshape((X, rows) + array.shape[1:])
        blocks = jnp.swapaxes(blocks, 1, 2).reshape((X * heads * rows,) + array.shape[2:])
        return head_exchange(blocks)

    q = by_rows(main_queries)
    lse = by_rows(main_lse) * log2e
    iq = by_rows(index_queries)
    w = by_rows(index_weights)
    lse = jnp.broadcast_to(lse[:, None], (lse.shape[0], BLOCK))
    w = jnp.broadcast_to(w[:, None], (w.shape[0], BLOCK))

    start = ctx_place * shard + head_place * rows
    qg, wg, kg = fused(start, y_place * C + core, q, lse, iq, iq.T, w, keys, rows)

    other = [(i, i ^ 1) for i in range(ctx_count)]
    sent = lax.dynamic_index_in_dim(kg, 1 - core, 0, keepdims=False)
    kept = lax.dynamic_index_in_dim(kg, core, 0, keepdims=False)
    came = lax.ppermute(sent, "ctx", other)
    part = (kept.astype(f32) + came.astype(f32)).astype(bf16)
    part = lax.all_to_all(part, "ctx", 0, 0, tiled=True, axis_index_groups=ctx_groups("y"))
    part = jnp.sum(part.astype(f32), axis=0)
    loss = jnp.broadcast_to(jnp.sum(part[Z * BLOCK, :]), (Z, 8, BLOCK))
    part = jnp.concatenate([part[: Z * BLOCK].reshape(Z, BLOCK, BLOCK), loss], axis=1)
    part = lax.all_to_all(part, "ctx", 0, 0, tiled=True, axis_index_groups=ctx_groups("z"))
    part = jnp.sum(part, axis=0)
    loss = jnp.broadcast_to(part[BLOCK:], (X, 8, BLOCK))
    part = jnp.concatenate([part[:BLOCK].T.reshape(X, rows, BLOCK), loss], axis=1)
    part = jnp.sum(head_exchange(part), axis=0)
    key_grads = part[:rows]
    loss = part[rows, 0] / all_tokens

    def by_heads(array):
        heads = array.shape[0] // rows // X
        back = head_exchange(array).reshape((X, heads, rows) + array.shape[1:])
        return jnp.swapaxes(back, 1, 2).reshape((shard, heads) + array.shape[1:])

    query_grads = by_heads(qg)
    weight_grads = by_heads(jnp.sum(wg, axis=1))
    return (loss, query_grads, weight_grads, key_grads)


def solution(mesh):
    return jax.shard_map(
        per_device,
        mesh=mesh,
        in_specs=(
            P("ctx", "head", None),
            P("ctx", None),
            P("ctx", "head"),
            P("ctx", "head", None),
            P("ctx", None),
            P("ctx", "head"),
        ),
        out_specs=(P(), P("ctx", "head", None), P("ctx", "head"), P(("ctx", "head"), None)),
        check_vma=False,
    )
```

```python
import functools
import math

import jax
import jax.numpy as jnp
from jax import lax
from jax.experimental import pallas as pl
from jax.experimental.pallas import tpu as pltpu
from jax.sharding import Mesh
from jax.sharding import PartitionSpec as P

f32, bf16 = jnp.float32, jnp.bfloat16
log2e = math.log2(math.e)
scale2 = 192.0 ** (-0.5) * log2e
far_below = -1e30

Y, Z, C, X = 4, 8, 2, 4
BLOCK = 128
KB = 512
STEPS = Z * Y * C * BLOCK // KB
UNROLL = 4
GROUPS = 2
ROWS = 16
LOSS_ROWS = 16
HEAD_CHUNK = 32
IHEAD_CHUNK = 32


def wide(column):
    return jnp.concatenate([column] * (KB // BLOCK), axis=1)


def column_place(info, column):
    pair, second = column // 2, column % 2
    offset = jnp.where(second == 0, Z - pair, jnp.where(pair == 0, Z // 2, pair))
    return (info[2] + offset) % Z


def y_place(info, index):
    return (info[1] + index) % Y


def step_facts(info, step, group):
    pair, y = step // Y, y_place(info, step % Y)
    first = (y * Z + column_place(info, 2 * pair)) * (C * BLOCK)
    second = (y * Z + column_place(info, 2 * pair + 1)) * (C * BLOCK)
    start = jnp.where(group == 0, info[0], info[4])
    needed = jnp.minimum(first, second) < start + ROWS
    lane = lax.broadcasted_iota(jnp.int32, (ROWS, KB), 1)
    base = jnp.where(lane < C * BLOCK, first, second)
    core = jnp.where(lane % (C * BLOCK) < BLOCK, info[3], 1 - info[3])
    key_pos = base + core * BLOCK + lane % BLOCK
    row_pos = start + lax.broadcasted_iota(jnp.int32, (ROWS, KB), 0)
    return needed, key_pos <= row_pos


def step_block(cols, step, first, last):
    pair, y = step // Y, step % Y
    return jnp.concatenate(
        [cols[2 * pair + i, side, y, first:last, :] for i in range(2) for side in range(C)],
        axis=1,
    )


def score_step(info, step, group, block, q_ref, lse_ref, iq_ref, w_ref, masses, logits, tops):
    heads, _, latent = q_ref.shape[1:]
    iheads = iq_ref.shape[1] // ROWS
    needed, visible = step_facts(info, step, group)

    @pl.when(needed)
    def compute():
        lat = block(0, latent)
        total = jnp.zeros((ROWS, KB), f32)
        for part in range(heads // HEAD_CHUNK):
            at = pl.ds(part * HEAD_CHUNK * ROWS, HEAD_CHUNK * ROWS)
            queries = q_ref[group, pl.ds(part * HEAD_CHUNK, HEAD_CHUNK)]
            queries = queries.reshape(HEAD_CHUNK * ROWS, latent)
            scores = jnp.dot(queries, lat, preferred_element_type=f32)
            mass = jnp.exp2(scores * scale2 - wide(lse_ref[group, at, :]))
            total = total + jnp.sum(mass.reshape(HEAD_CHUNK, ROWS, KB), axis=0)
        masses[group, step] = jnp.where(visible, total, 0.0)
        keys = block(latent, latent + BLOCK)
        logit = jnp.zeros((ROWS, KB), f32)
        for part in range(iheads // IHEAD_CHUNK):
            at = pl.ds(part * IHEAD_CHUNK * ROWS, IHEAD_CHUNK * ROWS)
            raw = jnp.dot(iq_ref[group, at, :], keys, preferred_element_type=f32)
            term = wide(w_ref[group, at, :]) * jnp.maximum(raw, 0.0)
            logit = logit + jnp.sum(term.reshape(IHEAD_CHUNK, ROWS, KB), axis=0)
        logit = jnp.where(visible, logit, far_below)
        logits[group, step] = logit
        tops[group] = jnp.maximum(tops[group], logit)

    @pl.when(jnp.logical_not(needed))
    def skip():
        masses[group, step] = jnp.zeros((ROWS, KB), f32)
        logits[group, step] = jnp.full((ROWS, KB), far_below, f32)


def column_copies(column_refs, cols, sems):
    copies = []
    for column, pieces in enumerate(column_refs):
        group = []
        for side, part in enumerate(pieces):
            at = 0
            for i, piece in enumerate(part):
                size = piece.shape[0]
                group.append(
                    pltpu.make_async_copy(
                        piece, cols.at[column, side, pl.ds(at, size)], sems.at[column, side, i]
                    )
                )
                at += size
        copies.append(group)
    return copies


def kernel(info, lse_ref, iq_ref, w_ref, iqt_ref, *refs):
    query_refs, refs = refs[:GROUPS], refs[GROUPS:]
    column_refs = [((refs[2 * k],), (refs[2 * k + 1],)) for k in range(Z - 1)]
    far, refs = refs[2 * (Z - 1) : 2 * (Z - 1) + 4], refs[2 * (Z - 1) + 4 :]
    column_refs.insert(1, ((far[0], far[1]), (far[2], far[3])))
    rows_ref, kept_ref, sent_ref, q_all, masses, logits, tops, scales, key_grads, wg_ref = refs[:10]
    cols, sems, q_sems = refs[10:]
    latent = q_all.shape[-1]
    per = q_all.shape[1] // X
    iheads = iq_ref.shape[1] // ROWS
    copies = column_copies(column_refs, cols, sems)
    query_copies = [
        pltpu.make_async_copy(
            source.at[x, pl.ds(0, per)], q_all.at[group, pl.ds(x * per, per)], q_sems.at[group, x]
        )
        for group, source in enumerate(query_refs)
        for x in range(X)
    ]
    for copy in query_copies:
        copy.start()
    for group in copies:
        for copy in group:
            copy.start()
    own_rows = iheads // X * ROWS
    rows_ref[...] = jnp.zeros(rows_ref.shape, f32)
    wg_ref[...] = jnp.zeros(wg_ref.shape, f32)
    tops[...] = jnp.full(tops.shape, far_below, f32)
    for copy in query_copies:
        copy.wait()

    def first_step(step, carried):
        for pair in range(Z // 2):

            @pl.when(step == pair * Y)
            def arrive():
                for copy in copies[2 * pair] + copies[2 * pair + 1]:
                    copy.wait()

        block = functools.partial(step_block, cols, step)

        def one_group(group, carried):
            score_step(
                info, step, group, block, q_all, lse_ref, iq_ref, w_ref, masses, logits, tops
            )
            return carried

        return lax.fori_loop(0, GROUPS, one_group, carried)

    lax.fori_loop(0, STEPS, first_step, 0)

    loss = jnp.float32(0.0)
    for group in range(GROUPS):
        top = jnp.max(tops[group], axis=1, keepdims=True)

        def exp_step(kb, carried):
            mass_sum, exp_sum, cross = carried
            for i in range(UNROLL):
                at = kb * UNROLL + i
                mass, logit = masses[group, at], logits[group, at]
                power = jnp.exp(logit - top)
                logits[group, at] = power
                mass_sum = mass_sum + mass
                exp_sum = exp_sum + power
                cross = cross + mass * logit
            return mass_sum, exp_sum, cross

        none = jnp.zeros((ROWS, KB), f32)
        sums = lax.fori_loop(0, STEPS // UNROLL, exp_step, (none, none, none))
        mass_sum, exp_sum, cross = [jnp.sum(part, axis=1, keepdims=True) for part in sums]
        scales[group, 0] = jnp.broadcast_to(1.0 / mass_sum, (ROWS, BLOCK))
        scales[group, 1] = jnp.broadcast_to(1.0 / exp_sum, (ROWS, BLOCK))
        loss = loss + jnp.sum(top + jnp.log(exp_sum) - cross / mass_sum)

    def second_step(kb, carried):
        key_grads[...] = jnp.zeros((BLOCK, KB), f32)

        def one_group(group, carried):
            needed, _ = step_facts(info, kb, group)

            @pl.when(needed)
            def compute():
                keys = step_block(cols, kb, latent, latent + BLOCK)
                target = masses[group, kb] * wide(scales[group, 0])
                coefficient = logits[group, kb] * wide(scales[group, 1]) - target
                coefficient = coefficient.astype(bf16).astype(f32)
                for part in range(iheads // IHEAD_CHUNK):
                    at = pl.ds(part * IHEAD_CHUNK * ROWS, IHEAD_CHUNK * ROWS)
                    raw = jnp.dot(iq_ref[group, at, :], keys, preferred_element_type=f32)
                    raw = raw.reshape(IHEAD_CHUNK, ROWS, KB)
                    weight = wide(w_ref[group, at, :]).reshape(IHEAD_CHUNK, ROWS, KB)
                    add = coefficient[None] * jnp.maximum(raw, 0.0)
                    add = add.reshape(IHEAD_CHUNK * ROWS, KB)
                    add = sum(add[:, i * BLOCK : (i + 1) * BLOCK] for i in range(KB // BLOCK))
                    wg_ref[group, at, :] += add
                    mixed = jnp.where(raw > 0.0, coefficient[None] * weight, 0.0).astype(bf16)
                    mixed = mixed.reshape(IHEAD_CHUNK * ROWS, KB)
                    grads = lax.dot_general(
                        mixed, keys, (((1,), (1,)), ((), ())), preferred_element_type=f32
                    )
                    for i in range(IHEAD_CHUNK * ROWS // own_rows):
                        x = part * (IHEAD_CHUNK * ROWS // own_rows) + i
                        grad = grads[i * own_rows : (i + 1) * own_rows]
                        rows_ref[x, group, 0:own_rows, :] += grad
                    key_grads[...] += jnp.dot(
                        iqt_ref[group, :, at], mixed, preferred_element_type=f32
                    )

            return carried

        carried = lax.fori_loop(0, GROUPS, one_group, carried)
        for i in range(2):
            z = column_place(info, 2 * (kb // Y) + i)
            at = pl.ds(pl.multiple_of(z * BLOCK, BLOCK), BLOCK)
            for side, ref in enumerate((kept_ref, sent_ref)):
                lanes = (i * C + side) * BLOCK
                ref[kb % Y, at, :] = key_grads[:, lanes : lanes + BLOCK].astype(bf16)
        return carried

    lax.fori_loop(0, STEPS, second_step, 0)

    for x in range(X):
        for group in range(GROUPS):
            sums = jnp.sum(wg_ref[group, x * own_rows : (x + 1) * own_rows, :].T, axis=0)
            rows_ref[x, group, own_rows:, :] = jnp.broadcast_to(sums[None], (8, own_rows))

    lane = lax.broadcasted_iota(jnp.int32, (LOSS_ROWS, BLOCK), 1)
    slot = (info[1] * C + info[3]) * 3
    high = loss.astype(bf16).astype(f32)
    middle = (loss - high).astype(bf16).astype(f32)
    low = loss - high - middle
    piece = jnp.where(lane == slot, high, 0.0)
    piece = piece + jnp.where(lane == slot + 1, middle, 0.0)
    piece = piece + jnp.where(lane == slot + 2, low, 0.0)
    for ref in (kept_ref, sent_ref):
        for y in range(Y):
            ref[y, Z * BLOCK :, :] = piece.astype(bf16)


vmem_spec = pl.BlockSpec(memory_space=pltpu.VMEM)
smem_spec = pl.BlockSpec(memory_space=pltpu.SMEM)
any_spec = pl.BlockSpec(memory_space=pl.ANY)
vmem_limit = 56 * 2**20


def fused(info, lse, iq, w, queries, heads, columns, far):
    piece = columns[0][0]
    latent = queries[0].shape[-1]
    flat = [array for pair in columns for array in pair] + [a for pair in far for a in pair]
    return pl.pallas_call(
        kernel,
        out_shape=(
            jax.ShapeDtypeStruct((X, GROUPS, iq.shape[1] // X + 8, BLOCK), f32),
            jax.ShapeDtypeStruct((Y, Z * BLOCK + LOSS_ROWS, BLOCK), bf16),
            jax.ShapeDtypeStruct((Y, Z * BLOCK + LOSS_ROWS, BLOCK), bf16),
        ),
        in_specs=[smem_spec] + [vmem_spec] * 4 + [any_spec] * (len(flat) + GROUPS),
        out_specs=(vmem_spec,) * 3,
        scratch_shapes=[
            pltpu.VMEM((GROUPS, heads, ROWS, latent), bf16),
            pltpu.VMEM((GROUPS, STEPS, ROWS, KB), f32),
            pltpu.VMEM((GROUPS, STEPS, ROWS, KB), f32),
            pltpu.VMEM((GROUPS, ROWS, KB), f32),
            pltpu.VMEM((GROUPS, 2, ROWS, BLOCK), f32),
            pltpu.VMEM((BLOCK, KB), f32),
            pltpu.VMEM(iq.shape, f32),
            pltpu.VMEM((Z, C) + piece.shape, bf16),
            pltpu.SemaphoreType.DMA((Z, C, 2)),
            pltpu.SemaphoreType.DMA((GROUPS, X)),
        ],
        compiler_params=pltpu.CompilerParams(vmem_limit_bytes=vmem_limit),
        name="fused",
    )(info, lse, iq, w, jnp.swapaxes(iq, 1, 2), *queries, *flat)


def ring(axis, size, offset):
    return lambda array: lax.ppermute(
        array, axis, [(i, (i + offset) % size) for i in range(size)]
    )


def head_exchange(array):
    return lax.all_to_all(array, "head", 0, 0, tiled=True)


def terms(array):
    high = lax.reduce_precision(array, 8, 7)
    middle = lax.reduce_precision(array - high, 8, 7)
    low = array - high - middle
    return [part.astype(bf16) for part in (high, middle, low)]


def per_device(main_queries, latents, main_lse, index_queries, index_keys, index_weights):
    shard, heads, latent = main_queries.shape
    iheads = index_queries.shape[1]
    all_tokens = shard * Y * Z * C
    y, z, core, head = (lax.axis_index(name) for name in ("y", "z", "core", "head"))

    def first_token(y):
        return ((y * Z + z) * C + core) * shard

    start = first_token(y) + head * ROWS
    mirror_start = first_token(Y - 1 - y) + shard // 2 + head * ROWS
    info = jnp.stack([start, y, z, core, mirror_start]).astype(jnp.int32)
    up, down, swap = ring("z", Z, 1), ring("z", Z, -1), ring("core", C, 1)

    def mirror(array):
        return lax.ppermute(array, "y", [(i, Y - 1 - i) for i in range(Y)])

    extra = [index_queries.reshape(shard, -1)] + terms(main_lse) + terms(index_weights)
    used = sum(part.shape[1] for part in extra)
    more = -(-used // latent)
    extra.append(jnp.zeros((shard, more * latent - used), bf16))
    extra = jnp.concatenate(extra, axis=1).reshape(shard, more, latent)
    packed = jnp.concatenate([main_queries, extra], axis=1)
    packed = packed.reshape(GROUPS, X, ROWS, heads + more, latent)
    packed = jnp.swapaxes(packed, 2, 3)
    packed = (head_exchange(packed[0]), head_exchange(mirror(packed[1])))
    extra = jnp.stack([part[:, heads:] for part in packed])
    extra = jnp.swapaxes(extra, 2, 3).reshape(GROUPS, X, ROWS, more * latent)

    def column_of(first, count):
        part = extra[..., first : first + 3 * count].astype(f32)
        part = part.reshape(GROUPS, X, ROWS, 3, count)
        part = part[..., 0, :] + part[..., 1, :] + part[..., 2, :]
        part = jnp.swapaxes(part, 2, 3).reshape(GROUPS, -1, 1)
        return part

    size = iheads * BLOCK
    iq = extra[..., :size].reshape(GROUPS, X, ROWS, iheads, BLOCK)
    iq = jnp.swapaxes(iq, 2, 3).reshape(GROUPS, -1, BLOCK)
    lse = column_of(size, heads) * log2e
    w = column_of(size + 3 * heads, iheads)
    lse = jnp.broadcast_to(lse, lse.shape[:2] + (BLOCK,))
    w = jnp.broadcast_to(w, w.shape[:2] + (BLOCK,))

    own = jnp.concatenate([latents, index_keys], axis=1).T
    column = jnp.stack(
        [own, ring("y", Y, -1)(own), ring("y", Y, 2)(own), ring("y", Y, 1)(own)]
    )
    columns = [column]
    above = below = column
    for _ in range(Z // 2 - 1):
        below, above = up(below), down(above)
        columns += [below, above]
    far = (up(below[: Y // 2]), down(above[Y // 2 :]))
    pairs = [(array, swap(array)) for array in columns]
    far = (far, tuple(swap(array) for array in far))

    row_grads, kept, sent = fused(info, lse, iq, w, packed, heads * X, pairs, far)

    per = iheads * ROWS
    back = head_exchange(row_grads)
    mirrored = mirror(back[:, 1])
    query_grads = jnp.stack([back[:, 0, :per], mirrored[:, :per]])
    query_grads = query_grads.reshape(GROUPS, X, iheads, ROWS, BLOCK)
    query_grads = jnp.swapaxes(query_grads, 2, 3).reshape(shard, iheads, BLOCK)
    weight_grads = jnp.stack([back[:, 0, per], mirrored[:, per]])
    weight_grads = weight_grads.reshape(GROUPS, X, iheads, ROWS)
    weight_grads = jnp.swapaxes(weight_grads, 2, 3).reshape(shard, iheads)

    rows = shard // X
    came = swap(sent)
    parts = [(kept[i].astype(f32) + came[i].astype(f32)).astype(bf16) for i in range(Y)]
    parts = [parts[0]] + [ring("y", Y, i)(parts[i]) for i in range(1, Y)]
    part = sum(array.astype(f32) for array in parts)
    loss = jnp.sum(part[Z * BLOCK, :]) + 0.0 * back[0, 0, 0, 0]
    part = jnp.swapaxes(part[: Z * BLOCK].reshape(Z, BLOCK, BLOCK), 1, 2)
    part = part.reshape(Z * X, rows, BLOCK)
    loss = jnp.broadcast_to(loss, (Z * X, 8, BLOCK))
    part = jnp.concatenate([part, loss], axis=1)
    part = lax.all_to_all(part, ("z", "head"), 0, 0, tiled=True)
    part = jnp.sum(part, axis=0)
    key_grads = part[:rows]
    loss = part[rows, 0] / all_tokens
    return (loss, query_grads, weight_grads, key_grads)


def solution(mesh):
    places = Mesh(mesh.devices.reshape(Y, Z, C, X), ("y", "z", "core", "head"))
    ctx = ("y", "z", "core")
    return jax.shard_map(
        per_device,
        mesh=places,
        in_specs=(
            P(ctx, "head", None),
            P(ctx, None),
            P(ctx, "head"),
            P(ctx, "head", None),
            P(ctx, None),
            P(ctx, "head"),
        ),
        out_specs=(P(), P(ctx, "head", None), P(ctx, "head"), P(ctx + ("head",), None)),
        check_vma=False,
    )
```

```python
import functools
import math

import jax
import jax.numpy as jnp
from jax import lax
from jax.experimental import pallas as pl
from jax.experimental.pallas import tpu as pltpu
from jax.sharding import Mesh
from jax.sharding import PartitionSpec as P

f32, bf16 = jnp.float32, jnp.bfloat16
log2e = math.log2(math.e)
scale2 = 192.0 ** (-0.5) * log2e
far_below = -1e30

Y, Z, C, X = 4, 8, 2, 4
BLOCK = 128
KB = 512
STEPS = Z * Y * C * BLOCK // KB
EARLY = (Z // 2 - 1) * Y
UNROLL = 4
GROUPS = 2
ROWS = 16
LOSS_ROWS = 16
HEAD_CHUNK = 32
IHEAD_CHUNK = 32


def wide(column):
    return jnp.concatenate([column] * (KB // BLOCK), axis=1)


def column_place(info, column):
    pair, second = column // 2, column % 2
    near = jnp.where(second == 0, Z - 1 - pair, pair + 1)
    offset = jnp.where(pair == Z // 2 - 1, second * (Z // 2), near)
    return (info[2] + offset) % Z


def y_place(info, index):
    return (info[1] + index) % Y


def step_facts(info, step, group):
    pair, y = step // Y, y_place(info, step % Y)
    first = (y * Z + column_place(info, 2 * pair)) * (C * BLOCK)
    second = (y * Z + column_place(info, 2 * pair + 1)) * (C * BLOCK)
    start = jnp.where(group == 0, info[0], info[4])
    needed = jnp.minimum(first, second) < start + ROWS
    lane = lax.broadcasted_iota(jnp.int32, (ROWS, KB), 1)
    base = jnp.where(lane < C * BLOCK, first, second)
    core = jnp.where(lane % (C * BLOCK) < BLOCK, info[3], 1 - info[3])
    key_pos = base + core * BLOCK + lane % BLOCK
    row_pos = start + lax.broadcasted_iota(jnp.int32, (ROWS, KB), 0)
    return needed, key_pos <= row_pos


def step_block(cols, step, first, last):
    pair, y = step // Y, step % Y
    return jnp.concatenate(
        [cols[2 * pair + i, side, y, first:last, :] for i in range(2) for side in range(C)],
        axis=1,
    )


def score_step(info, step, base, group, block, q_ref, lse_ref, iq_ref, w_ref, masses, logits, tops):
    heads, _, latent = q_ref.shape[1:]
    iheads = iq_ref.shape[1] // ROWS
    needed, visible = step_facts(info, base + step, group)

    @pl.when(needed)
    def compute():
        lat = block(0, latent)
        total = jnp.zeros((ROWS, KB), f32)
        for part in range(heads // HEAD_CHUNK):
            at = pl.ds(part * HEAD_CHUNK * ROWS, HEAD_CHUNK * ROWS)
            queries = q_ref[group, pl.ds(part * HEAD_CHUNK, HEAD_CHUNK)]
            queries = queries.reshape(HEAD_CHUNK * ROWS, latent)
            scores = jnp.dot(queries, lat, preferred_element_type=f32)
            mass = jnp.exp2(scores * scale2 - wide(lse_ref[group, at, :]))
            total = total + jnp.sum(mass.reshape(HEAD_CHUNK, ROWS, KB), axis=0)
        masses[group, step] = jnp.where(visible, total, 0.0)
        keys = block(latent, latent + BLOCK)
        logit = jnp.zeros((ROWS, KB), f32)
        for part in range(iheads // IHEAD_CHUNK):
            at = pl.ds(part * IHEAD_CHUNK * ROWS, IHEAD_CHUNK * ROWS)
            raw = jnp.dot(iq_ref[group, at, :], keys, preferred_element_type=f32)
            term = wide(w_ref[group, at, :]) * jnp.maximum(raw, 0.0)
            logit = logit + jnp.sum(term.reshape(IHEAD_CHUNK, ROWS, KB), axis=0)
        logit = jnp.where(visible, logit, far_below)
        logits[group, step] = logit
        tops[group] = jnp.maximum(tops[group], logit)

    @pl.when(jnp.logical_not(needed))
    def skip():
        masses[group, step] = jnp.zeros((ROWS, KB), f32)
        logits[group, step] = jnp.full((ROWS, KB), far_below, f32)


def arrivals(query_refs, column_refs, q_all, cols, sems, q_sems):
    per = q_all.shape[1] // X
    queries = [
        pltpu.make_async_copy(
            source.at[x, pl.ds(0, per)], q_all.at[group, pl.ds(x * per, per)], q_sems.at[group, x]
        )
        for group, source in enumerate(query_refs)
        for x in range(X)
    ]
    columns = [
        pltpu.make_async_copy(ref, cols.at[i // C, i % C], sems.at[i // C, i % C])
        for i, ref in enumerate(column_refs)
    ]
    for copy in queries + columns[: 2 * C]:
        copy.start()
    return queries, columns


def score_steps(info, base, columns, cols, q_all, lse_ref, iq_ref, w_ref, masses, logits, tops):
    per_pair = 2 * C

    def step(index, carried):
        for pair in range(len(columns) // per_pair):

            @pl.when(index == pair * Y)
            def arrive():
                for copy in columns[pair * per_pair : (pair + 1) * per_pair]:
                    copy.wait()

        block = functools.partial(step_block, cols, index)

        def one_group(group, carried):
            score_step(
                info, index, base, group, block, q_all, lse_ref, iq_ref, w_ref, masses, logits, tops
            )
            return carried

        return lax.fori_loop(0, GROUPS, one_group, carried)

    lax.fori_loop(0, len(columns) // per_pair * Y, step, 0)


def early_kernel(info, lse_ref, iq_ref, w_ref, *refs):
    query_refs, column_refs, refs = refs[:GROUPS], refs[GROUPS:-8], refs[-8:]
    masses, logits, tops, keys_ref, q_all, cols, sems, q_sems = refs
    latent = q_all.shape[-1]
    queries, columns = arrivals(query_refs, column_refs, q_all, cols, sems, q_sems)
    tops[...] = jnp.full(tops.shape, far_below, f32)
    for copy in queries:
        copy.wait()
    for copy in columns[2 * C :]:
        copy.start()
    score_steps(info, 0, columns, cols, q_all, lse_ref, iq_ref, w_ref, masses, logits, tops)

    def keep_keys(step, carried):
        keys_ref[step] = step_block(cols, step, latent, latent + BLOCK)
        return carried

    lax.fori_loop(0, EARLY, keep_keys, 0)


def late_kernel(info, lse_ref, iq_ref, w_ref, iqt_ref, early_tops, *refs):
    query_refs, column_refs, refs = refs[:GROUPS], refs[GROUPS : GROUPS + 2 * C], refs[GROUPS + 2 * C :]
    early_refs, refs = refs[:3], refs[3:]
    rows_ref, kept_ref, sent_ref, q_all, masses, logits, tops, scales, key_grads, wg_ref = refs[:10]
    keys_all, cols, sems, q_sems, early_sems = refs[10:]
    latent = q_all.shape[-1]
    iheads = iq_ref.shape[1] // ROWS
    queries, columns = arrivals(query_refs, column_refs, q_all, cols, sems, q_sems)
    early_copies = [
        pltpu.make_async_copy(source, target, early_sems.at[i])
        for i, (source, target) in enumerate(
            zip(
                early_refs,
                (
                    masses.at[:, pl.ds(0, EARLY)],
                    logits.at[:, pl.ds(0, EARLY)],
                    keys_all.at[pl.ds(0, EARLY)],
                ),
            )
        )
    ]
    own_rows = iheads // X * ROWS
    rows_ref[...] = jnp.zeros(rows_ref.shape, f32)
    wg_ref[...] = jnp.zeros(wg_ref.shape, f32)
    tops[...] = early_tops[...]
    for copy in queries:
        copy.wait()
    for copy in early_copies:
        copy.start()
    score_steps(
        info, EARLY, columns, cols, q_all, lse_ref, iq_ref, w_ref,
        masses.at[:, pl.ds(EARLY, Y)], logits.at[:, pl.ds(EARLY, Y)], tops,
    )
    for step in range(Y):
        keys_all[EARLY + step] = step_block(cols, step, latent, latent + BLOCK)
    for copy in early_copies:
        copy.wait()

    loss = jnp.float32(0.0)
    for group in range(GROUPS):
        top = jnp.max(tops[group], axis=1, keepdims=True)

        def exp_step(kb, carried):
            mass_sum, exp_sum, cross = carried
            for i in range(UNROLL):
                at = kb * UNROLL + i
                mass, logit = masses[group, at], logits[group, at]
                power = jnp.exp(logit - top)
                logits[group, at] = power
                mass_sum = mass_sum + mass
                exp_sum = exp_sum + power
                cross = cross + mass * logit
            return mass_sum, exp_sum, cross

        none = jnp.zeros((ROWS, KB), f32)
        sums = lax.fori_loop(0, STEPS // UNROLL, exp_step, (none, none, none))
        mass_sum, exp_sum, cross = [jnp.sum(part, axis=1, keepdims=True) for part in sums]
        scales[group, 0] = jnp.broadcast_to(1.0 / mass_sum, (ROWS, BLOCK))
        scales[group, 1] = jnp.broadcast_to(1.0 / exp_sum, (ROWS, BLOCK))
        loss = loss + jnp.sum(top + jnp.log(exp_sum) - cross / mass_sum)

    def second_step(kb, carried):
        key_grads[...] = jnp.zeros((BLOCK, KB), f32)

        def one_group(group, carried):
            needed, _ = step_facts(info, kb, group)

            @pl.when(needed)
            def compute():
                keys = keys_all[kb]
                target = masses[group, kb] * wide(scales[group, 0])
                coefficient = logits[group, kb] * wide(scales[group, 1]) - target
                coefficient = coefficient.astype(bf16).astype(f32)
                for part in range(iheads // IHEAD_CHUNK):
                    at = pl.ds(part * IHEAD_CHUNK * ROWS, IHEAD_CHUNK * ROWS)
                    raw = jnp.dot(iq_ref[group, at, :], keys, preferred_element_type=f32)
                    raw = raw.reshape(IHEAD_CHUNK, ROWS, KB)
                    weight = wide(w_ref[group, at, :]).reshape(IHEAD_CHUNK, ROWS, KB)
                    add = coefficient[None] * jnp.maximum(raw, 0.0)
                    add = add.reshape(IHEAD_CHUNK * ROWS, KB)
                    add = sum(add[:, i * BLOCK : (i + 1) * BLOCK] for i in range(KB // BLOCK))
                    wg_ref[group, at, :] += add
                    mixed = jnp.where(raw > 0.0, coefficient[None] * weight, 0.0).astype(bf16)
                    mixed = mixed.reshape(IHEAD_CHUNK * ROWS, KB)
                    grads = lax.dot_general(
                        mixed, keys, (((1,), (1,)), ((), ())), preferred_element_type=f32
                    )
                    for i in range(IHEAD_CHUNK * ROWS // own_rows):
                        x = part * (IHEAD_CHUNK * ROWS // own_rows) + i
                        grad = grads[i * own_rows : (i + 1) * own_rows]
                        rows_ref[x, group, 0:own_rows, :] += grad
                    key_grads[...] += jnp.dot(
                        iqt_ref[group, :, at], mixed, preferred_element_type=f32
                    )

            return carried

        carried = lax.fori_loop(0, GROUPS, one_group, carried)
        for i in range(2):
            z = column_place(info, 2 * (kb // Y) + i)
            at = pl.ds(pl.multiple_of(z * BLOCK, BLOCK), BLOCK)
            for side, ref in enumerate((kept_ref, sent_ref)):
                lanes = (i * C + side) * BLOCK
                ref[kb % Y, at, :] = key_grads[:, lanes : lanes + BLOCK].astype(bf16)
        return carried

    lax.fori_loop(0, STEPS, second_step, 0)

    for x in range(X):
        for group in range(GROUPS):
            sums = jnp.sum(wg_ref[group, x * own_rows : (x + 1) * own_rows, :].T, axis=0)
            rows_ref[x, group, own_rows:, :] = jnp.broadcast_to(sums[None], (8, own_rows))

    lane = lax.broadcasted_iota(jnp.int32, (LOSS_ROWS, BLOCK), 1)
    slot = (info[1] * C + info[3]) * 3
    high = loss.astype(bf16).astype(f32)
    middle = (loss - high).astype(bf16).astype(f32)
    low = loss - high - middle
    piece = jnp.where(lane == slot, high, 0.0)
    piece = piece + jnp.where(lane == slot + 1, middle, 0.0)
    piece = piece + jnp.where(lane == slot + 2, low, 0.0)
    for ref in (kept_ref, sent_ref):
        for y in range(Y):
            ref[y, Z * BLOCK :, :] = piece.astype(bf16)


vmem_spec = pl.BlockSpec(memory_space=pltpu.VMEM)
smem_spec = pl.BlockSpec(memory_space=pltpu.SMEM)
any_spec = pl.BlockSpec(memory_space=pl.ANY)
vmem_limit = 56 * 2**20


def call(body, info, small, queries, heads, columns, more, out_shape, scratch, flops, name):
    count = len(columns) // C
    latent = queries[0].shape[-1]
    any_count = GROUPS + len(columns) + len(more)
    return pl.pallas_call(
        body,
        out_shape=out_shape,
        in_specs=[smem_spec] + [vmem_spec] * len(small) + [any_spec] * any_count,
        out_specs=(vmem_spec,) * len(out_shape),
        scratch_shapes=[pltpu.VMEM((GROUPS, heads, ROWS, latent), bf16)]
        + scratch
        + [
            pltpu.VMEM((count, C) + columns[0].shape, bf16),
            pltpu.SemaphoreType.DMA((count, C)),
            pltpu.SemaphoreType.DMA((GROUPS, X)),
        ]
        + ([pltpu.SemaphoreType.DMA((len(more),))] if more else []),
        compiler_params=pltpu.CompilerParams(vmem_limit_bytes=vmem_limit),
        cost_estimate=pl.CostEstimate(flops=flops, bytes_accessed=16 * 2**20, transcendentals=0),
        name=name,
    )(info, *small, *queries, *columns, *more)


def fused(info, lse, iq, w, queries, heads, pairs):
    flat = [array for pair in pairs for array in pair]
    columns = flat[2 * C :] + flat[: 2 * C]
    early_columns, late_columns = columns[: EARLY // Y * 2 * C], columns[EARLY // Y * 2 * C :]
    step_flops = 2 * KB * (heads * GROUPS * ROWS * queries[0].shape[-1] + iq.size)
    early = call(
        early_kernel,
        info,
        (lse, iq, w),
        queries,
        heads,
        early_columns,
        (),
        (
            jax.ShapeDtypeStruct((GROUPS, EARLY, ROWS, KB), f32),
            jax.ShapeDtypeStruct((GROUPS, EARLY, ROWS, KB), f32),
            jax.ShapeDtypeStruct((GROUPS, ROWS, KB), f32),
            jax.ShapeDtypeStruct((EARLY, BLOCK, KB), bf16),
        ),
        [],
        EARLY * step_flops,
        "early",
    )
    masses, logits, tops, keys = early
    return call(
        late_kernel,
        info,
        (lse, iq, w, jnp.swapaxes(iq, 1, 2), tops),
        queries,
        heads,
        late_columns,
        (masses, logits, keys),
        (
            jax.ShapeDtypeStruct((X, GROUPS, iq.shape[1] // X + 8, BLOCK), f32),
            jax.ShapeDtypeStruct((Y, Z * BLOCK + LOSS_ROWS, BLOCK), bf16),
            jax.ShapeDtypeStruct((Y, Z * BLOCK + LOSS_ROWS, BLOCK), bf16),
        ),
        [
            pltpu.VMEM((GROUPS, STEPS, ROWS, KB), f32),
            pltpu.VMEM((GROUPS, STEPS, ROWS, KB), f32),
            pltpu.VMEM((GROUPS, ROWS, KB), f32),
            pltpu.VMEM((GROUPS, 2, ROWS, BLOCK), f32),
            pltpu.VMEM((BLOCK, KB), f32),
            pltpu.VMEM(iq.shape, f32),
            pltpu.VMEM((STEPS, BLOCK, KB), bf16),
        ],
        Y * step_flops + 3 * STEPS * 2 * KB * iq.size,
        "late",
    )


def ring(axis, size, offset):
    return lambda array: lax.ppermute(
        array, axis, [(i, (i + offset) % size) for i in range(size)]
    )


def head_exchange(array):
    return lax.all_to_all(array, "head", 0, 0, tiled=True)


def terms(array):
    high = lax.reduce_precision(array, 8, 7)
    middle = lax.reduce_precision(array - high, 8, 7)
    low = array - high - middle
    return [part.astype(bf16) for part in (high, middle, low)]


def per_device(main_queries, latents, main_lse, index_queries, index_keys, index_weights):
    shard, heads, latent = main_queries.shape
    iheads = index_queries.shape[1]
    all_tokens = shard * Y * Z * C
    y, z, core, head = (lax.axis_index(name) for name in ("y", "z", "core", "head"))

    def first_token(y):
        return ((y * Z + z) * C + core) * shard

    start = first_token(y) + head * ROWS
    mirror_start = first_token(Y - 1 - y) + shard // 2 + head * ROWS
    info = jnp.stack([start, y, z, core, mirror_start]).astype(jnp.int32)
    up, down, swap = ring("z", Z, 1), ring("z", Z, -1), ring("core", C, 1)

    def mirror(array):
        return lax.ppermute(array, "y", [(i, Y - 1 - i) for i in range(Y)])

    own = jnp.concatenate([latents, index_keys], axis=1).T
    around = [ring("y", Y, -1)(own), ring("y", Y, 2)(own), ring("y", Y, 1)(own)]
    column = jnp.stack([own] + around)
    after = jnp.max(column[:, 0, :]) * 0.0

    extra = [index_queries.reshape(shard, -1)] + terms(main_lse) + terms(index_weights)
    used = sum(part.shape[1] for part in extra)
    more = -(-used // latent)
    extra.append(jnp.zeros((shard, more * latent - used), bf16))
    extra = jnp.concatenate(extra, axis=1).reshape(shard, more, latent)

    packed = jnp.concatenate([main_queries, extra], axis=1)
    packed = packed.reshape(GROUPS, X, ROWS, heads + more, latent)
    packed = jnp.swapaxes(packed, 2, 3)
    packed = (head_exchange(packed[0]), head_exchange(mirror(packed[1] + after)))
    extra = jnp.stack([part[:, heads:] for part in packed])
    extra = jnp.swapaxes(extra, 2, 3).reshape(GROUPS, X, ROWS, more * latent)

    def column_of(first, count):
        part = extra[..., first : first + 3 * count].astype(f32)
        part = part.reshape(GROUPS, X, ROWS, 3, count)
        part = part[..., 0, :] + part[..., 1, :] + part[..., 2, :]
        part = jnp.swapaxes(part, 2, 3).reshape(GROUPS, -1, 1)
        return part

    size = iheads * BLOCK
    iq = extra[..., :size].reshape(GROUPS, X, ROWS, iheads, BLOCK)
    iq = jnp.swapaxes(iq, 2, 3).reshape(GROUPS, -1, BLOCK)
    lse = column_of(size, heads) * log2e
    w = column_of(size + 3 * heads, iheads)
    lse = jnp.broadcast_to(lse, lse.shape[:2] + (BLOCK,))
    w = jnp.broadcast_to(w, w.shape[:2] + (BLOCK,))

    columns = [column]
    above = below = column
    for _ in range(Z // 2 - 1):
        below, above = up(below), down(above)
        columns += [below, above]
    pairs = [(array, swap(array)) for array in columns]
    pairs.insert(1, (up(below), down(pairs[-1][1])))

    row_grads, kept, sent = fused(info, lse, iq, w, packed, heads * X, pairs)

    per = iheads * ROWS
    back = head_exchange(row_grads)
    mirrored = mirror(back[:, 1])
    query_grads = jnp.stack([back[:, 0, :per], mirrored[:, :per]])
    query_grads = query_grads.reshape(GROUPS, X, iheads, ROWS, BLOCK)
    query_grads = jnp.swapaxes(query_grads, 2, 3).reshape(shard, iheads, BLOCK)
    weight_grads = jnp.stack([back[:, 0, per], mirrored[:, per]])
    weight_grads = weight_grads.reshape(GROUPS, X, iheads, ROWS)
    weight_grads = jnp.swapaxes(weight_grads, 2, 3).reshape(shard, iheads)

    rows = shard // X
    came = swap(sent)
    parts = [(kept[i].astype(f32) + came[i].astype(f32)).astype(bf16) for i in range(Y)]
    parts = [parts[0]] + [ring("y", Y, i)(parts[i]) for i in range(1, Y)]
    part = sum(array.astype(f32) for array in parts)
    loss = part[Z * BLOCK, :] + 0.0 * back[0, 0, 0, 0]
    part = jnp.swapaxes(part[: Z * BLOCK].reshape(Z, BLOCK, BLOCK), 1, 2)
    part = part.reshape(Z * X, rows, BLOCK).astype(bf16)
    loss = jnp.pad(jnp.stack(terms(loss)), ((0, LOSS_ROWS - 3), (0, 0)))
    loss = jnp.broadcast_to(loss, (Z * X, LOSS_ROWS, BLOCK))
    part = jnp.concatenate([part, loss], axis=1)
    part = lax.all_to_all(part, ("z", "head"), 0, 0, tiled=True)
    part = jnp.sum(part.astype(f32), axis=0)
    key_grads = part[:rows]
    loss = jnp.sum(part[rows:]) / all_tokens
    return (loss, query_grads, weight_grads, key_grads)


def solution(mesh):
    places = Mesh(mesh.devices.reshape(Y, Z, C, X), ("y", "z", "core", "head"))
    ctx = ("y", "z", "core")
    return jax.shard_map(
        per_device,
        mesh=places,
        in_specs=(
            P(ctx, "head", None),
            P(ctx, None),
            P(ctx, "head"),
            P(ctx, "head", None),
            P(ctx, None),
            P(ctx, "head"),
        ),
        out_specs=(P(), P(ctx, "head", None), P(ctx, "head"), P(ctx + ("head",), None)),
        check_vma=False,
    )
```

```python
import functools
import math

import jax
import jax.numpy as jnp
from jax import lax
from jax.experimental import pallas as pl
from jax.experimental.pallas import tpu as pltpu
from jax.sharding import Mesh
from jax.sharding import PartitionSpec as P

f32, bf16 = jnp.float32, jnp.bfloat16
log2e = math.log2(math.e)
scale2 = 192.0 ** (-0.5) * log2e
far_below = -1e30

Y, Z, C, X = 4, 8, 2, 4
BLOCK = 128
KB = 512
STEPS = Z * Y * C * BLOCK // KB
EARLY = (Z // 2 - 1) * Y
UNROLL = 4
GROUPS = 2
ROWS = 16
LOSS_ROWS = 16
HEAD_CHUNK = 32
IHEAD_CHUNK = 32


def wide(column):
    return jnp.concatenate([column] * (KB // BLOCK), axis=1)


def column_place(info, column):
    pair, second = column // 2, column % 2
    near = jnp.where(second == 0, Z - 1 - pair, pair + 1)
    offset = jnp.where(pair == Z // 2 - 1, second * (Z // 2), near)
    return (info[2] + offset) % Z


def y_place(info, index):
    return (info[1] + index) % Y


def step_facts(info, step, group):
    pair, y = step // Y, y_place(info, step % Y)
    first = (y * Z + column_place(info, 2 * pair)) * (C * BLOCK)
    second = (y * Z + column_place(info, 2 * pair + 1)) * (C * BLOCK)
    start = jnp.where(group == 0, info[0], info[4])
    needed = jnp.minimum(first, second) < start + ROWS
    lane = lax.broadcasted_iota(jnp.int32, (ROWS, KB), 1)
    base = jnp.where(lane < C * BLOCK, first, second)
    core = jnp.where(lane % (C * BLOCK) < BLOCK, info[3], 1 - info[3])
    key_pos = base + core * BLOCK + lane % BLOCK
    row_pos = start + lax.broadcasted_iota(jnp.int32, (ROWS, KB), 0)
    return needed, key_pos <= row_pos


def step_block(cols, step, first, last):
    pair, y = step // Y, step % Y
    return jnp.concatenate(
        [cols[2 * pair + i, side, y, first:last, :] for i in range(2) for side in range(C)],
        axis=1,
    )


def score_step(info, step, base, group, block, q_ref, lse_ref, iq_ref, w_ref, masses, logits, tops):
    heads, _, latent = q_ref.shape[1:]
    iheads = iq_ref.shape[1] // ROWS
    needed, visible = step_facts(info, base + step, group)

    @pl.when(needed)
    def compute():
        lat = block(0, latent)
        total = jnp.zeros((ROWS, KB), f32)
        for part in range(heads // HEAD_CHUNK):
            at = pl.ds(part * HEAD_CHUNK * ROWS, HEAD_CHUNK * ROWS)
            queries = q_ref[group, pl.ds(part * HEAD_CHUNK, HEAD_CHUNK)]
            queries = queries.reshape(HEAD_CHUNK * ROWS, latent)
            scores = jnp.dot(queries, lat, preferred_element_type=f32)
            mass = jnp.exp2(scores * scale2 - wide(lse_ref[group, at, :]))
            total = total + jnp.sum(mass.reshape(HEAD_CHUNK, ROWS, KB), axis=0)
        masses[group, step] = jnp.where(visible, total, 0.0)
        keys = block(latent, latent + BLOCK)
        logit = jnp.zeros((ROWS, KB), f32)
        for part in range(iheads // IHEAD_CHUNK):
            at = pl.ds(part * IHEAD_CHUNK * ROWS, IHEAD_CHUNK * ROWS)
            raw = jnp.dot(iq_ref[group, at, :], keys, preferred_element_type=f32)
            term = wide(w_ref[group, at, :]) * jnp.maximum(raw, 0.0)
            logit = logit + jnp.sum(term.reshape(IHEAD_CHUNK, ROWS, KB), axis=0)
        logit = jnp.where(visible, logit, far_below)
        logits[group, step] = logit
        tops[group] = jnp.maximum(tops[group], logit)

    @pl.when(jnp.logical_not(needed))
    def skip():
        masses[group, step] = jnp.zeros((ROWS, KB), f32)
        logits[group, step] = jnp.full((ROWS, KB), far_below, f32)


def arrivals(query_refs, column_refs, q_all, cols, sems, q_sems):
    per = q_all.shape[1] // X
    queries = [
        pltpu.make_async_copy(
            source.at[x, pl.ds(0, per)], q_all.at[group, pl.ds(x * per, per)], q_sems.at[group, x]
        )
        for group, source in enumerate(query_refs)
        for x in range(X)
    ]
    columns = [
        pltpu.make_async_copy(ref, cols.at[i // C, i % C], sems.at[i // C, i % C])
        for i, ref in enumerate(column_refs)
    ]
    for copy in queries + columns[: 2 * C]:
        copy.start()
    return queries, columns


def score_steps(info, base, columns, cols, q_all, lse_ref, iq_ref, w_ref, masses, logits, tops):
    per_pair = 2 * C

    def step(index, carried):
        for pair in range(len(columns) // per_pair):

            @pl.when(index == pair * Y)
            def arrive():
                for copy in columns[pair * per_pair : (pair + 1) * per_pair]:
                    copy.wait()

        block = functools.partial(step_block, cols, index)

        def one_group(group, carried):
            score_step(
                info, index, base, group, block, q_all, lse_ref, iq_ref, w_ref, masses, logits, tops
            )
            return carried

        return lax.fori_loop(0, GROUPS, one_group, carried)

    lax.fori_loop(0, len(columns) // per_pair * Y, step, 0)


def spread(source, target):
    for group in range(GROUPS):
        for i in range(source.shape[1]):
            block = jnp.broadcast_to(source[group, i : i + 1, :], (BLOCK, BLOCK))
            target[group, i * BLOCK : (i + 1) * BLOCK, :] = block.T


def early_kernel(info, lse_in, iq_ref, w_in, *refs):
    query_refs, column_refs, refs = refs[:GROUPS], refs[GROUPS:-10], refs[-10:]
    masses, logits, tops, keys_ref, q_all, lse_ref, w_ref, cols, sems, q_sems = refs
    latent = q_all.shape[-1]
    queries, columns = arrivals(query_refs, column_refs, q_all, cols, sems, q_sems)
    spread(lse_in, lse_ref)
    spread(w_in, w_ref)
    tops[...] = jnp.full(tops.shape, far_below, f32)
    for copy in queries:
        copy.wait()
    for copy in columns[2 * C :]:
        copy.start()
    score_steps(info, 0, columns, cols, q_all, lse_ref, iq_ref, w_ref, masses, logits, tops)

    def keep_keys(step, carried):
        keys_ref[step] = step_block(cols, step, latent, latent + BLOCK)
        return carried

    lax.fori_loop(0, EARLY, keep_keys, 0)


def late_kernel(info, lse_in, iq_ref, w_in, iqt_ref, early_tops, *refs):
    query_refs, column_refs, refs = refs[:GROUPS], refs[GROUPS : GROUPS + 2 * C], refs[GROUPS + 2 * C :]
    early_refs, refs = refs[:3], refs[3:]
    rows_ref, kept_ref, sent_ref, q_all, masses, logits, tops, scales, key_grads, wg_ref = refs[:10]
    keys_all, lse_ref, w_ref, cols, sems, q_sems, early_sems = refs[10:]
    latent = q_all.shape[-1]
    iheads = iq_ref.shape[1] // ROWS
    queries, columns = arrivals(query_refs, column_refs, q_all, cols, sems, q_sems)
    early_copies = [
        pltpu.make_async_copy(source, target, early_sems.at[i])
        for i, (source, target) in enumerate(
            zip(
                early_refs,
                (
                    masses.at[:, pl.ds(0, EARLY)],
                    logits.at[:, pl.ds(0, EARLY)],
                    keys_all.at[pl.ds(0, EARLY)],
                ),
            )
        )
    ]
    own_rows = iheads // X * ROWS
    rows_ref[...] = jnp.zeros(rows_ref.shape, f32)
    wg_ref[...] = jnp.zeros(wg_ref.shape, f32)
    spread(lse_in, lse_ref)
    spread(w_in, w_ref)
    tops[...] = early_tops[...]
    for copy in queries:
        copy.wait()
    for copy in early_copies:
        copy.start()
    score_steps(
        info, EARLY, columns, cols, q_all, lse_ref, iq_ref, w_ref,
        masses.at[:, pl.ds(EARLY, Y)], logits.at[:, pl.ds(EARLY, Y)], tops,
    )
    for step in range(Y):
        keys_all[EARLY + step] = step_block(cols, step, latent, latent + BLOCK)
    for copy in early_copies:
        copy.wait()

    loss = jnp.float32(0.0)
    for group in range(GROUPS):
        top = jnp.max(tops[group], axis=1, keepdims=True)

        def exp_step(kb, carried):
            mass_sum, exp_sum, cross = carried
            for i in range(UNROLL):
                at = kb * UNROLL + i
                mass, logit = masses[group, at], logits[group, at]
                power = jnp.exp(logit - top)
                logits[group, at] = power
                mass_sum = mass_sum + mass
                exp_sum = exp_sum + power
                cross = cross + mass * logit
            return mass_sum, exp_sum, cross

        none = jnp.zeros((ROWS, KB), f32)
        sums = lax.fori_loop(0, STEPS // UNROLL, exp_step, (none, none, none))
        mass_sum, exp_sum, cross = [jnp.sum(part, axis=1, keepdims=True) for part in sums]
        scales[group, 0] = jnp.broadcast_to(1.0 / mass_sum, (ROWS, BLOCK))
        scales[group, 1] = jnp.broadcast_to(1.0 / exp_sum, (ROWS, BLOCK))
        loss = loss + jnp.sum(top + jnp.log(exp_sum) - cross / mass_sum)

    def second_step(kb, carried):
        key_grads[...] = jnp.zeros((BLOCK, KB), f32)

        def one_group(group, carried):
            needed, _ = step_facts(info, kb, group)

            @pl.when(needed)
            def compute():
                keys = keys_all[kb]
                target = masses[group, kb] * wide(scales[group, 0])
                coefficient = logits[group, kb] * wide(scales[group, 1]) - target
                coefficient = coefficient.astype(bf16).astype(f32)
                for part in range(iheads // IHEAD_CHUNK):
                    at = pl.ds(part * IHEAD_CHUNK * ROWS, IHEAD_CHUNK * ROWS)
                    raw = jnp.dot(iq_ref[group, at, :], keys, preferred_element_type=f32)
                    raw = raw.reshape(IHEAD_CHUNK, ROWS, KB)
                    weight = wide(w_ref[group, at, :]).reshape(IHEAD_CHUNK, ROWS, KB)
                    add = coefficient[None] * jnp.maximum(raw, 0.0)
                    add = add.reshape(IHEAD_CHUNK * ROWS, KB)
                    add = sum(add[:, i * BLOCK : (i + 1) * BLOCK] for i in range(KB // BLOCK))
                    wg_ref[group, at, :] += add
                    mixed = jnp.where(raw > 0.0, coefficient[None] * weight, 0.0).astype(bf16)
                    mixed = mixed.reshape(IHEAD_CHUNK * ROWS, KB)
                    grads = lax.dot_general(
                        mixed, keys, (((1,), (1,)), ((), ())), preferred_element_type=f32
                    )
                    for i in range(IHEAD_CHUNK * ROWS // own_rows):
                        x = part * (IHEAD_CHUNK * ROWS // own_rows) + i
                        grad = grads[i * own_rows : (i + 1) * own_rows]
                        rows_ref[x, group, 0:own_rows, :] += grad
                    key_grads[...] += jnp.dot(
                        iqt_ref[group, :, at], mixed, preferred_element_type=f32
                    )

            return carried

        carried = lax.fori_loop(0, GROUPS, one_group, carried)
        for i in range(2):
            z = column_place(info, 2 * (kb // Y) + i)
            at = pl.ds(pl.multiple_of(z * BLOCK, BLOCK), BLOCK)
            for side, ref in enumerate((kept_ref, sent_ref)):
                lanes = (i * C + side) * BLOCK
                ref[kb % Y, at, :] = key_grads[:, lanes : lanes + BLOCK].astype(bf16)
        return carried

    lax.fori_loop(0, STEPS, second_step, 0)

    for x in range(X):
        for group in range(GROUPS):
            sums = jnp.sum(wg_ref[group, x * own_rows : (x + 1) * own_rows, :].T, axis=0)
            rows_ref[x, group, own_rows:, :] = jnp.broadcast_to(sums[None], (8, own_rows))

    lane = lax.broadcasted_iota(jnp.int32, (LOSS_ROWS, BLOCK), 1)
    slot = (info[1] * C + info[3]) * 3
    high = loss.astype(bf16).astype(f32)
    middle = (loss - high).astype(bf16).astype(f32)
    low = loss - high - middle
    piece = jnp.where(lane == slot, high, 0.0)
    piece = piece + jnp.where(lane == slot + 1, middle, 0.0)
    piece = piece + jnp.where(lane == slot + 2, low, 0.0)
    for ref in (kept_ref, sent_ref):
        for y in range(Y):
            ref[y, Z * BLOCK :, :] = piece.astype(bf16)


vmem_spec = pl.BlockSpec(memory_space=pltpu.VMEM)
smem_spec = pl.BlockSpec(memory_space=pltpu.SMEM)
any_spec = pl.BlockSpec(memory_space=pl.ANY)
vmem_limit = 56 * 2**20


def call(body, info, small, queries, heads, columns, more, out_shape, scratch, flops, name):
    count = len(columns) // C
    latent = queries[0].shape[-1]
    any_count = GROUPS + len(columns) + len(more)
    return pl.pallas_call(
        body,
        out_shape=out_shape,
        in_specs=[smem_spec] + [vmem_spec] * len(small) + [any_spec] * any_count,
        out_specs=(vmem_spec,) * len(out_shape),
        scratch_shapes=[pltpu.VMEM((GROUPS, heads, ROWS, latent), bf16)]
        + scratch
        + [
            pltpu.VMEM((count, C) + columns[0].shape, bf16),
            pltpu.SemaphoreType.DMA((count, C)),
            pltpu.SemaphoreType.DMA((GROUPS, X)),
        ]
        + ([pltpu.SemaphoreType.DMA((len(more),))] if more else []),
        compiler_params=pltpu.CompilerParams(vmem_limit_bytes=vmem_limit),
        cost_estimate=pl.CostEstimate(flops=flops, bytes_accessed=16 * 2**20, transcendentals=0),
        name=name,
    )(info, *small, *queries, *columns, *more)


def fused(info, lse, iq, w, queries, heads, pairs):
    flat = [array for pair in pairs for array in pair]
    columns = flat[2 * C :] + flat[: 2 * C]
    early_columns, late_columns = columns[: EARLY // Y * 2 * C], columns[EARLY // Y * 2 * C :]
    step_flops = 2 * KB * (heads * GROUPS * ROWS * queries[0].shape[-1] + iq.size)
    spaces = [
        pltpu.VMEM((GROUPS, heads * ROWS, BLOCK), f32),
        pltpu.VMEM(iq.shape, f32),
    ]
    early = call(
        early_kernel,
        info,
        (lse, iq, w),
        queries,
        heads,
        early_columns,
        (),
        (
            jax.ShapeDtypeStruct((GROUPS, EARLY, ROWS, KB), f32),
            jax.ShapeDtypeStruct((GROUPS, EARLY, ROWS, KB), f32),
            jax.ShapeDtypeStruct((GROUPS, ROWS, KB), f32),
            jax.ShapeDtypeStruct((EARLY, BLOCK, KB), bf16),
        ),
        spaces,
        EARLY * step_flops,
        "early",
    )
    masses, logits, tops, keys = early
    return call(
        late_kernel,
        info,
        (lse, iq, w, jnp.swapaxes(iq, 1, 2), tops),
        queries,
        heads,
        late_columns,
        (masses, logits, keys),
        (
            jax.ShapeDtypeStruct((X, GROUPS, iq.shape[1] // X + 8, BLOCK), f32),
            jax.ShapeDtypeStruct((Y, Z * BLOCK + LOSS_ROWS, BLOCK), bf16),
            jax.ShapeDtypeStruct((Y, Z * BLOCK + LOSS_ROWS, BLOCK), bf16),
        ),
        [
            pltpu.VMEM((GROUPS, STEPS, ROWS, KB), f32),
            pltpu.VMEM((GROUPS, STEPS, ROWS, KB), f32),
            pltpu.VMEM((GROUPS, ROWS, KB), f32),
            pltpu.VMEM((GROUPS, 2, ROWS, BLOCK), f32),
            pltpu.VMEM((BLOCK, KB), f32),
            pltpu.VMEM(iq.shape, f32),
            pltpu.VMEM((STEPS, BLOCK, KB), bf16),
        ]
        + spaces,
        Y * step_flops + 3 * STEPS * 2 * KB * iq.size,
        "late",
    )


def ring(axis, size, offset):
    return lambda array: lax.ppermute(
        array, axis, [(i, (i + offset) % size) for i in range(size)]
    )


def head_exchange(array):
    return lax.all_to_all(array, "head", 0, 0, tiled=True)


def terms(array):
    high = lax.reduce_precision(array, 8, 7)
    middle = lax.reduce_precision(array - high, 8, 7)
    low = array - high - middle
    return [part.astype(bf16) for part in (high, middle, low)]


def per_device(main_queries, latents, main_lse, index_queries, index_keys, index_weights):
    shard, heads, latent = main_queries.shape
    iheads = index_queries.shape[1]
    all_tokens = shard * Y * Z * C
    y, z, core, head = (lax.axis_index(name) for name in ("y", "z", "core", "head"))

    def first_token(y):
        return ((y * Z + z) * C + core) * shard

    start = first_token(y) + head * ROWS
    mirror_start = first_token(Y - 1 - y) + shard // 2 + head * ROWS
    info = jnp.stack([start, y, z, core, mirror_start]).astype(jnp.int32)
    up, down, swap = ring("z", Z, 1), ring("z", Z, -1), ring("core", C, 1)

    def mirror(array):
        return lax.ppermute(array, "y", [(i, Y - 1 - i) for i in range(Y)])

    own = jnp.concatenate([latents, index_keys], axis=1).T
    around = [ring("y", Y, -1)(own), ring("y", Y, 2)(own), ring("y", Y, 1)(own)]
    column = jnp.stack([own] + around)
    after = jnp.max(column[:, 0, :]) * 0.0

    extra = [index_queries.reshape(shard, -1)] + terms(main_lse) + terms(index_weights)
    used = sum(part.shape[1] for part in extra)
    more = -(-used // latent)
    extra.append(jnp.zeros((shard, more * latent - used), bf16))
    extra = jnp.concatenate(extra, axis=1).reshape(shard, more, latent)

    packed = jnp.concatenate([main_queries, extra], axis=1)
    packed = packed.reshape(GROUPS, X, ROWS, heads + more, latent)
    packed = jnp.swapaxes(packed, 2, 3)
    packed = (head_exchange(packed[0]), head_exchange(mirror(packed[1] + after)))
    extra = jnp.stack([part[:, heads:] for part in packed])
    extra = jnp.swapaxes(extra, 2, 3).reshape(GROUPS, X, ROWS, more * latent)

    def column_of(first, count):
        part = extra[..., first : first + 3 * count].astype(f32)
        part = part.reshape(GROUPS, X, ROWS, 3, count)
        part = part[..., 0, :] + part[..., 1, :] + part[..., 2, :]
        part = jnp.swapaxes(part, 2, 3).reshape(GROUPS, -1, BLOCK)
        return part

    size = iheads * BLOCK
    iq = extra[..., :size].reshape(GROUPS, X, ROWS, iheads, BLOCK)
    iq = jnp.swapaxes(iq, 2, 3).reshape(GROUPS, -1, BLOCK)
    lse = column_of(size, heads) * log2e
    w = column_of(size + 3 * heads, iheads)

    columns = [column]
    above = below = column
    for _ in range(Z // 2 - 1):
        below, above = up(below), down(above)
        columns += [below, above]
    pairs = [(array, swap(array)) for array in columns]
    pairs.insert(1, (up(below), down(pairs[-1][1])))

    row_grads, kept, sent = fused(info, lse, iq, w, packed, heads * X, pairs)

    per = iheads * ROWS
    back = head_exchange(row_grads)
    mirrored = mirror(back[:, 1])
    query_grads = jnp.stack([back[:, 0, :per], mirrored[:, :per]])
    query_grads = query_grads.reshape(GROUPS, X, iheads, ROWS, BLOCK)
    query_grads = jnp.swapaxes(query_grads, 2, 3).reshape(shard, iheads, BLOCK)
    weight_grads = jnp.stack([back[:, 0, per], mirrored[:, per]])
    weight_grads = weight_grads.reshape(GROUPS, X, iheads, ROWS)
    weight_grads = jnp.swapaxes(weight_grads, 2, 3).reshape(shard, iheads)

    rows = shard // X
    came = swap(sent)
    parts = [(kept[i].astype(f32) + came[i].astype(f32)).astype(bf16) for i in range(Y)]
    parts = [parts[0]] + [ring("y", Y, i)(parts[i]) for i in range(1, Y)]
    part = sum(array.astype(f32) for array in parts)
    loss = part[Z * BLOCK, :] + 0.0 * back[0, 0, 0, 0]
    part = jnp.swapaxes(part[: Z * BLOCK].reshape(Z, BLOCK, BLOCK), 1, 2)
    part = part.reshape(Z * X, rows, BLOCK).astype(bf16)
    loss = jnp.pad(jnp.stack(terms(loss)), ((0, LOSS_ROWS - 3), (0, 0)))
    loss = jnp.broadcast_to(loss, (Z * X, LOSS_ROWS, BLOCK))
    part = jnp.concatenate([part, loss], axis=1)
    part = lax.all_to_all(part, ("z", "head"), 0, 0, tiled=True)
    part = jnp.sum(part.astype(f32), axis=0)
    key_grads = part[:rows]
    loss = jnp.sum(part[rows:]) / all_tokens
    return (loss, query_grads, weight_grads, key_grads)


def solution(mesh):
    places = Mesh(mesh.devices.reshape(Y, Z, C, X), ("y", "z", "core", "head"))
    ctx = ("y", "z", "core")
    return jax.shard_map(
        per_device,
        mesh=places,
        in_specs=(
            P(ctx, "head", None),
            P(ctx, None),
            P(ctx, "head"),
            P(ctx, "head", None),
            P(ctx, None),
            P(ctx, "head"),
        ),
        out_specs=(P(), P(ctx, "head", None), P(ctx, "head"), P(ctx + ("head",), None)),
        check_vma=False,
    )
```
